32 devices in a mesh: chain: 2 (over y), gx: 4 (over z), gy: 4 (over x, core).
Axes of the slice: x: 2, y: 2, z: 4, core: 2. Of those that a mesh axis runs over, the one named last changes fastest.
Arguments:
- pressure: float32 [64, 512, 256], P(('chain', 'gx'), 'gy'), parts along dimension 0, may hold values from -3 to 3
- adjoint: float32 [64, 512, 256], P(('chain', 'gx'), 'gy'), parts along dimension 0, may hold values from -3 to 3
- log_perm: float32 [64, 512, 256], P(('chain', 'gx'), 'gy'), parts along dimension 0, may hold values from -3 to 3
- phi_x: float32 [32, 32], P('gx'), may hold values from -1 to 1
- phi_y: float32 [512, 32], P('gy'), may hold values from -0.25 to 0.25
- phi_z: float32 [256, 16], replicated, may hold values from -0.375 to 0.375
- obs_cells: int32 [3, 8192], P(None, 'chain'), parts along dimension 1, may hold values from 0 to 511, as said below
- core_values: float32 [8192], P('chain'), parts along dimension 0, may hold values from -4 to 4
Outputs:
- coeff_grad: float32 [64, 32, 16], P(('chain', 'gx'), 'gy'), parts along dimension 0
The draws below stay inside these ranges and needn't reach their ends.
There are 2 independent parts, one for each index of `chain`. The reference program is written for one: setup_inputs(seed, part) draws one part's arguments, and reference() takes and returns one part's arrays. A program takes and returns all parts, laid end to end along the dimension named above; an argument that names none is the same for every part. Nothing has to cross between parts.
Inputs may be any that keep to these rules, and one draw needn't show every extreme that they name: `obs_cells`: row 0 holds x cells below 32, row 1 y cells below 512, row 2 z cells below 256; cells may repeat.
All inputs are finite; a program needn't handle non-finite values.
Results may differ from the reference program's by a relative error of at most 0.000071.
Values sent between devices are 32-bit elements; how exact they have to be, the bound alone decides.
A program may use at most 64 MiB of HBM per device.

```python
import jax
import jax.numpy as jnp
from jax import lax

NZ = 256
MX = 32
MY = 32
MZ = 16
OBS = 4096
NX = 32
NY = 512


def draw_obs_cells(key, part):
    key = jax.random.fold_in(key, 7)
    keys = jax.random.split(key, 3)
    along_x = jax.random.randint(keys[0], (OBS,), 0, NX)
    along_y = jax.random.randint(keys[1], (OBS,), 0, NY)
    along_z = jax.random.randint(keys[2], (OBS,), 0, NZ)
    along_x = along_x.at[0].set(NX - 1).at[1].set(0)
    along_y = along_y.at[0].set(NY - 1).at[1].set(0)
    along_z = along_z.at[0].set(NZ - 1).at[1].set(0)
    return jnp.stack([along_x, along_y, along_z]).astype(jnp.int32)


def shard_levels(own_key, extent, cuts, low, top_value):
    level = 1.0
    for axis_at, blocks in cuts:
        heights = jax.random.uniform(jax.random.fold_in(jax.random.fold_in(own_key, 6), axis_at), (blocks,), jnp.float32, low / len(cuts), top_value / len(cuts))
        level = level * jnp.repeat(jnp.exp(heights), extent[axis_at] // blocks).reshape((-1,) + (1,) * (len(extent) - 1 - axis_at))
    return level


def scatter_about(key, extent, scale, most, shards=(), kind=jnp.bfloat16):
    array = scale * jax.random.normal(key, extent, jnp.float32)
    if shards:
        array = array * shard_levels(key, extent, shards, -0.22, 0.18)
    return jnp.clip(array, -most, most).astype(kind)


def setup_inputs(seed: int = 0, part: int = 0) -> dict:
    streams_of = jax.random.split(jax.random.key(seed), 9)
    part_splits = jax.random.split(jax.random.fold_in(streams_of[8], part), 9)
    pressure = scatter_about(part_splits[0], (NX, NY, NZ), 0.5, 3.0, ((0, 4), (1, 4)), jnp.float32)
    adjoint = scatter_about(part_splits[1], (NX, NY, NZ), 0.5, 3.0, ((0, 4), (1, 4)), jnp.float32)
    log_perm = scatter_about(part_splits[2], (NX, NY, NZ), 0.7, 3.0, ((0, 4), (1, 4)), jnp.float32)
    phi_x = scatter_about(streams_of[3], (NX, MX), NX ** -0.5, 1.0, ((0, 4),), jnp.float32)
    phi_y = scatter_about(streams_of[4], (NY, MY), NY ** -0.5, 0.25, ((0, 4),), jnp.float32)
    phi_z = scatter_about(streams_of[5], (NZ, MZ), NZ ** -0.5, 0.375, (), jnp.float32)
    obs_cells = draw_obs_cells(jax.random.fold_in(jax.random.fold_in(streams_of[8], part), 71), part)
    core_values = scatter_about(part_splits[7], (OBS,), 1.0, 4.0, (), jnp.float32)
    return {"pressure": pressure, "adjoint": adjoint, "log_perm": log_perm, "phi_x": phi_x, "phi_y": phi_y, "phi_z": phi_z, "obs_cells": obs_cells, "core_values": core_values}


core_weight = 100.0


def paired_sum(faces, axis_dim):
    low = [(0, 0)] * 3
    high = [(0, 0)] * 3
    low[axis_dim] = (1, 0)
    high[axis_dim] = (0, 1)
    return jnp.pad(faces, low) + jnp.pad(faces, high)


def reference(pressure, adjoint, log_perm, phi_x, phi_y, phi_z, obs_cells, core_values):
    permeability = jnp.exp(log_perm)
    faces_x = (pressure[1:] - pressure[:-1]) * (adjoint[1:] - adjoint[:-1])
    faces_y = (pressure[:, 1:] - pressure[:, :-1]) * (adjoint[:, 1:] - adjoint[:, :-1])
    faces_z = (pressure[:, :, 1:] - pressure[:, :, :-1]) * (adjoint[:, :, 1:] - adjoint[:, :, :-1])
    face_total = paired_sum(faces_x, 0) + paired_sum(faces_y, 1) + paired_sum(faces_z, 2)
    cell_grad = -0.5 * permeability * face_total
    cell_x = obs_cells[0]
    cell_y = obs_cells[1]
    cell_z = obs_cells[2]
    misfit = core_weight * (log_perm[cell_x, cell_y, cell_z] - core_values)
    cell_grad = cell_grad.at[cell_x, cell_y, cell_z].add(-misfit)
    highest = lax.Precision.HIGHEST
    depth = cell_grad.shape[2]
    partial_value = jnp.dot(cell_grad.reshape(-1, depth), phi_z, precision=highest)
    partial_value = partial_value.reshape(cell_grad.shape[0], cell_grad.shape[1], phi_z.shape[1])
    partial_value = jnp.einsum("ijz,jb->ibz", partial_value, phi_y, precision=highest)
    return jnp.einsum("ibz,ia->abz", partial_value, phi_x, precision=highest)
```

```python
import functools

import jax
import jax.numpy as jnp
from jax import lax
from jax.experimental import pallas as pl
from jax.experimental.pallas import tpu as pltpu
from jax.sharding import PartitionSpec as P

core_weight = 100.0
TILE = 8
CHUNK = 512
f32, bf16 = jnp.float32, jnp.bfloat16
MESH = pl.DeviceIdType.MESH


def dot_nn(a, b):
    return lax.dot_general(a, b, (((1,), (0,)), ((), ())), preferred_element_type=f32)


def dot_nt(a, b):
    return lax.dot_general(a, b, (((1,), (1,)), ((), ())), preferred_element_type=f32)


def split(value):
    high = value.astype(bf16)
    return high, (value - high.astype(f32)).astype(bf16)


def one_hot(size, width, which):
    return jnp.where(lax.broadcasted_iota(jnp.int32, (size, width), 0) == which, 1.0, 0.0)


def each(count, step):
    if count <= 16:
        for i in range(count):
            step(i)
    else:
        lax.fori_loop(0, count, lambda i, c: (step(i), c)[1], 0)


def stacked(value):
    return jnp.concatenate(split(value), axis=0)


def kernel(
    n_gx, n_gy,
    p_in, a_in, lp_in, phix_in, phiy_in, phiz_in, obs_in, core_in,
    out_ref,
    p, a, lp, phix, phiy, phiz, obs, core,
    counts, cores, part, kron, pieces, landed,
    load_sems, halo_send, halo_recv, piece_send, piece_recv,
):
    rows, cols, depth = lp.shape
    mx, my, mz = phix.shape[1], phiy.shape[0], phiz.shape[0]
    share_x, share_y = mx // n_gx, my // n_gy
    width = share_x * mz
    gx, gy = lax.axis_index("gx"), lax.axis_index("gy")
    peers = n_gx * n_gy

    def peer(d):
        return lax.rem(gx + d // n_gy, n_gx), lax.rem(gy + d % n_gy, n_gy)

    barrier = pltpu.get_barrier_semaphore()

    def greet(d):
        tx, ty = peer(d + 1)
        pl.semaphore_signal(barrier, inc=1, device_id={"gx": tx, "gy": ty}, device_id_type=MESH)

    each(peers - 1, greet)

    inner = (pl.ds(1, rows), pl.ds(TILE, cols))
    loads = [
        pltpu.make_async_copy(src, dst, load_sems.at[i])
        for i, (src, dst) in enumerate(
            (
                (obs_in, obs),
                (core_in, core),
                (phix_in, phix),
                (phiy_in, phiy),
                (phiz_in, phiz),
                (p_in, p.at[inner]),
                (a_in, a.at[inner]),
                (lp_in, lp),
            )
        )
    ]
    for load in loads:
        load.start()

    pl.semaphore_wait(barrier, peers - 1)

    own_cols = pl.ds(TILE, cols)
    own_rows = pl.ds(1, rows)

    def halo(k, field, array, scratch):
        src, dst, target = (
            (array.at[rows - 1], scratch.at[0, own_cols], {"gx": gx + 1}),
            (array.at[0], scratch.at[rows + 1, own_cols], {"gx": gx - 1}),
            (
                array.at[:, pl.ds(cols - TILE, TILE)],
                scratch.at[own_rows, pl.ds(0, TILE)],
                {"gy": gy + 1},
            ),
            (
                array.at[:, pl.ds(0, TILE)],
                scratch.at[own_rows, pl.ds(cols + TILE, TILE)],
                {"gy": gy - 1},
            ),
        )[k]
        return pltpu.make_async_remote_copy(
            src_ref=src,
            dst_ref=dst,
            send_sem=halo_send.at[2 * k + field],
            recv_sem=halo_recv.at[2 * k + field],
            device_id=target,
            device_id_type=MESH,
        )

    fields = ((0, p_in, p), (1, a_in, a))
    sends = (gx < n_gx - 1, gx > 0, gy < n_gy - 1, gy > 0)
    gets = (gx > 0, gx < n_gx - 1, gy > 0, gy < n_gy - 1)
    for k in (0, 1, 2, 3):

        @pl.when(sends[k])
        def _(k=k):
            for field, array, scratch in fields:
                halo(k, field, array, scratch).start()

    for load in loads[:5]:
        load.wait()

    phiz_t = stacked(phiz[...])
    phiy_t = stacked(phiy[...])
    counts[...] = jnp.zeros_like(counts)
    cores[...] = jnp.zeros_like(cores)

    def observe(c, carry):
        at = pl.ds(pl.multiple_of(c * CHUNK, CHUNK), CHUNK)
        local_x = obs[0:1, at] - gx * rows
        in_y = one_hot(cols, CHUNK, obs[1:2, at] - gy * cols).astype(bf16)
        in_z = one_hot(depth, CHUNK, obs[2:3, at]).astype(bf16)
        in_x = [jnp.where(local_x == i, 1.0, 0.0).astype(bf16) for i in range(rows)]
        cells = jnp.concatenate([in_y * in_x[i] for i in range(rows)], axis=0)
        counts[...] += dot_nt(cells, in_z)
        both = dot_nn(phiz_t, in_z)
        high, low = split((both[:mz] + both[mz:]) * core[0:1, at])
        weighted = jnp.concatenate(
            [high * in_x[i] for i in range(rows)] + [low * in_x[i] for i in range(rows)], axis=0
        )
        cores[...] += dot_nt(weighted, in_y)
        return carry

    lax.fori_loop(0, obs.shape[1] // CHUNK, observe, 0)

    tall, wide = rows * mz, mx * mz
    spread_rows = jnp.where(
        lax.broadcasted_iota(jnp.int32, (tall, rows), 0) // mz
        == lax.broadcasted_iota(jnp.int32, (tall, rows), 1),
        1.0,
        0.0,
    ).astype(bf16)
    spread_cols = jnp.where(
        lax.broadcasted_iota(jnp.int32, (mx, wide), 1) // mz
        == lax.broadcasted_iota(jnp.int32, (mx, wide), 0),
        1.0,
        0.0,
    ).astype(bf16)
    same = lax.rem(lax.broadcasted_iota(jnp.int32, (tall, wide), 0), mz) == lax.rem(
        lax.broadcasted_iota(jnp.int32, (tall, wide), 1), mz
    )
    for i, half in enumerate(split(phix[...])):
        block = dot_nn(dot_nn(spread_rows, half).astype(bf16), spread_cols)
        kron[i] = jnp.where(same, block, 0.0).astype(bf16)

    for load in loads[5:]:
        load.wait()

    for k in (2, 3):
        @pl.when(gets[k])
        def _(k=k):
            for field, array, scratch in fields:
                halo(k, field, array, scratch).wait_recv()

        @pl.when(jnp.logical_not(gets[k]))
        def _(k=k):
            for _, _, scratch in fields:
                line = TILE if k == 2 else TILE + cols - 1
                place = 0 if k == 2 else TILE + cols
                for i in range(1, rows + 1):
                    scratch[i, place : place + TILE] = jnp.broadcast_to(
                        scratch[i, line : line + 1], (TILE, depth)
                    )

    def own(scratch, i):
        return scratch[i, TILE : TILE + cols]

    last = lax.broadcasted_iota(jnp.int32, (cols, depth), 1) == depth - 1

    def flat_faces(i):
        pc, ac = own(p, i), own(a, i)
        up = (pltpu.roll(pc, depth - 1, 1) - pc) * (pltpu.roll(ac, depth - 1, 1) - ac)
        up = jnp.where(last, 0.0, up)
        total = up + pltpu.roll(up, 1, 1)
        for s in (TILE - 1, TILE + 1):
            total += (p[i, s : s + cols] - pc) * (a[i, s : s + cols] - ac)
        return total

    def x_face(i, j):
        return (own(p, i) - own(p, j)) * (own(a, i) - own(a, j))

    def project(i, total):
        field = lp[i]
        cell = -0.5 * jnp.exp(field) * total - (core_weight * counts[i * cols : (i + 1) * cols]) * field
        high, low = split(cell)
        x = dot_nt(phiz_t, high)
        x = x[:mz] + x[mz:] + dot_nt(phiz_t[:mz], low)
        at = pl.ds(i * mz, mz)
        top = i * mz
        seen = cores[top : top + mz] + cores[tall + top : tall + top + mz]
        part[at] = x + core_weight * seen

    for i in range(1, rows - 1):
        project(i, flat_faces(i + 1) + x_face(i + 1, i) + x_face(i + 1, i + 2))
    edges = [flat_faces(1) + x_face(1, 2), flat_faces(rows) + x_face(rows, rows - 1)]

    for k in (0, 1):

        @pl.when(gets[k])
        def _(k=k):
            for field, array, scratch in fields:
                halo(k, field, array, scratch).wait_recv()

        @pl.when(jnp.logical_not(gets[k]))
        def _(k=k):
            for _, _, scratch in fields:
                scratch[(rows + 1) * k, TILE : TILE + cols] = own(scratch, 1 + (rows - 1) * k)

    project(0, edges[0] + x_face(1, 0))
    project(rows - 1, edges[1] + x_face(rows, rows + 1))

    high, low = split(part[...])
    y = dot_nt(phiy_t, high)
    y = y[:my] + y[my:] + dot_nt(phiy_t[:my], low)
    high, low = split(y)
    folded = dot_nn(high, kron[0]) + dot_nn(low, kron[0]) + dot_nn(high, kron[1])
    for i in range(n_gx):
        for j in range(n_gy):
            pieces[i, j] = folded[j * share_y : (j + 1) * share_y, i * width : (i + 1) * width]

    def piece(d):
        tx, ty = peer(d)
        return pltpu.make_async_remote_copy(
            src_ref=pieces.at[tx, ty],
            dst_ref=landed.at[d],
            send_sem=piece_send,
            recv_sem=piece_recv,
            device_id={"gx": tx, "gy": ty},
            device_id_type=MESH,
        )

    each(peers - 1, lambda d: piece(d + 1).start())
    landed[0] = pieces[gx, gy]
    rest = landed.at[pl.ds(1, peers - 1)]
    pltpu.make_async_copy(rest, rest, piece_recv).wait()
    out_ref[...] = jnp.sum(landed[...], axis=0)
    pltpu.make_async_copy(rest, rest, piece_send).wait()
    for k in (0, 1, 2, 3):

        @pl.when(sends[k])
        def _(k=k):
            for field, array, scratch in fields:
                halo(k, field, array, scratch).wait_send()


def body(pressure, adjoint, log_perm, phi_x, phi_y, phi_z, obs_cells, core_values):
    rows, cols, depth = pressure.shape
    n_gx, n_gy = lax.axis_size("gx"), lax.axis_size("gy")
    mx, my, mz = phi_x.shape[1], phi_y.shape[1], phi_z.shape[1]
    share_x, share_y = mx // n_gx, my // n_gy
    width = share_x * mz
    seen = core_values.shape[0]
    padded = (rows + 2, cols + 2 * TILE, depth)
    phi_y, phi_z = phi_y.T, phi_z.T
    cores = core_values.reshape(1, seen)
    args = (pressure, adjoint, log_perm, phi_x, phi_y, phi_z, obs_cells, cores)
    out = pl.pallas_call(
        functools.partial(kernel, n_gx, n_gy),
        out_shape=jax.ShapeDtypeStruct((share_y, width), f32),
        in_specs=[pl.BlockSpec(memory_space=pltpu.HBM)] * len(args),
        out_specs=pl.BlockSpec(memory_space=pltpu.VMEM),
        scratch_shapes=[
            pltpu.VMEM(padded, f32),
            pltpu.VMEM(padded, f32),
            pltpu.VMEM((rows, cols, depth), f32),
            pltpu.VMEM(phi_x.shape, f32),
            pltpu.VMEM(phi_y.shape, f32),
            pltpu.VMEM(phi_z.shape, f32),
            pltpu.VMEM(obs_cells.shape, jnp.int32),
            pltpu.VMEM((1, seen), f32),
            pltpu.VMEM((rows * cols, depth), f32),
            pltpu.VMEM((2 * rows * mz, cols), f32),
            pltpu.VMEM((rows * mz, cols), f32),
            pltpu.VMEM((2, rows * mz, mx * mz), bf16),
            pltpu.VMEM((n_gx, n_gy, share_y, width), f32),
            pltpu.VMEM((n_gx * n_gy, share_y, width), f32),
            pltpu.SemaphoreType.DMA((8,)),
            pltpu.SemaphoreType.DMA((8,)),
            pltpu.SemaphoreType.DMA((8,)),
            pltpu.SemaphoreType.DMA,
            pltpu.SemaphoreType.DMA,
        ],
        compiler_params=pltpu.CompilerParams(
            collective_id=0, has_side_effects=True, vmem_limit_bytes=63 * 1024 * 1024
        ),
    )(*args)
    return out.reshape(share_y, share_x, mz).transpose(1, 0, 2)


def solution(mesh):
    placed = (
        P(("chain", "gx"), "gy", None),
        P(("chain", "gx"), "gy", None),
        P(("chain", "gx"), "gy", None),
        P("gx", None),
        P("gy", None),
        P(),
        P(None, "chain"),
        P("chain"),
    )
    return jax.shard_map(
        body, mesh=mesh, in_specs=placed, out_specs=P(("chain", "gx"), "gy", None), check_vma=False
    )
```

```python
import functools

import jax
import jax.numpy as jnp
from jax import lax
from jax.experimental import pallas as pl
from jax.experimental.pallas import tpu as pltpu
from jax.sharding import PartitionSpec as P

core_weight = 100.0
TILE = 8
CHUNK = 512
f32, bf16 = jnp.float32, jnp.bfloat16
MESH = pl.DeviceIdType.MESH


def dot_nn(a, b):
    return lax.dot_general(a, b, (((1,), (0,)), ((), ())), preferred_element_type=f32)


def dot_nt(a, b):
    return lax.dot_general(a, b, (((1,), (1,)), ((), ())), preferred_element_type=f32)


def split(value):
    high = value.astype(bf16)
    return high, (value - high.astype(f32)).astype(bf16)


def one_hot(size, width, which):
    return jnp.where(lax.broadcasted_iota(jnp.int32, (size, width), 0) == which, 1.0, 0.0)


def each(count, step):
    if count <= 16:
        for i in range(count):
            step(i)
    else:
        lax.fori_loop(0, count, lambda i, c: (step(i), c)[1], 0)


def stacked(value):
    return jnp.concatenate(split(value), axis=0)


def kernel(
    n_gx, n_gy,
    p_in, a_in, lp_in, phix_in, phiy_in, phiz_in, obs_in, core_in,
    out_ref,
    p, a, lp, phix, phiy, phiz, obs, core,
    counts, cores, part, kron, leave, arrive, pieces, landed,
    load_sems, halo_send, halo_recv, piece_send, piece_recv, ready,
):
    rows, cols, depth = lp.shape
    mx, my, mz = phix.shape[1], phiy.shape[0], phiz.shape[0]
    share_x, share_y = mx // n_gx, my // n_gy
    width = share_x * mz
    gx, gy = lax.axis_index("gx"), lax.axis_index("gy")
    peers = n_gx * n_gy

    def peer(d):
        return lax.rem(gx + d // n_gy, n_gx), lax.rem(gy + d % n_gy, n_gy)

    inner = (pl.ds(1, rows), pl.ds(TILE, cols))
    loads = [
        pltpu.make_async_copy(src, dst, load_sems.at[i])
        for i, (src, dst) in enumerate(
            (
                (phix_in, phix),
                (p_in, p.at[inner]),
                (a_in, a.at[inner]),
                (phiy_in, phiy),
                (phiz_in, phiz),
                (obs_in, obs),
                (core_in, core),
                (lp_in, lp),
            )
        )
    ]
    barrier = pltpu.get_barrier_semaphore()

    def signal(semaphore, axis, size, d):
        target = {axis: lax.rem(lax.axis_index(axis) + d + 1, size)}
        pl.semaphore_signal(semaphore, inc=1, device_id=target, device_id_type=MESH)

    each(n_gx - 1, functools.partial(signal, barrier, "gx", n_gx))
    each(n_gy - 1, functools.partial(signal, barrier, "gy", n_gy))
    for load in loads:
        load.start()

    loads[0].wait()
    tall, wide = rows * mz, mx * mz
    spread_rows = jnp.where(
        lax.broadcasted_iota(jnp.int32, (tall, rows), 0) // mz
        == lax.broadcasted_iota(jnp.int32, (tall, rows), 1),
        1.0,
        0.0,
    ).astype(bf16)
    spread_cols = jnp.where(
        lax.broadcasted_iota(jnp.int32, (mx, wide), 1) // mz
        == lax.broadcasted_iota(jnp.int32, (mx, wide), 0),
        1.0,
        0.0,
    ).astype(bf16)
    same = lax.rem(lax.broadcasted_iota(jnp.int32, (tall, wide), 0), mz) == lax.rem(
        lax.broadcasted_iota(jnp.int32, (tall, wide), 1), mz
    )
    for i, half in enumerate(split(phix[...])):
        block = dot_nn(dot_nn(spread_rows, half).astype(bf16), spread_cols)
        kron[i] = jnp.where(same, block, 0.0).astype(bf16)
    loads[1].wait()
    loads[2].wait()
    for field, scratch in ((0, p), (1, a)):
        leave[0, field] = scratch[1 : rows + 1, TILE + cols - 1]
        leave[1, field] = scratch[1 : rows + 1, TILE]

    pl.semaphore_wait(barrier, n_gx + n_gy - 2)

    own_cols = pl.ds(TILE, cols)

    def halo(k, field, array, scratch):
        src, dst, target = (
            (array.at[rows - 1], scratch.at[0, own_cols], {"gx": gx + 1}),
            (array.at[0], scratch.at[rows + 1, own_cols], {"gx": gx - 1}),
            (leave.at[0, field], arrive.at[0, field], {"gy": gy + 1}),
            (leave.at[1, field], arrive.at[1, field], {"gy": gy - 1}),
        )[k]
        return pltpu.make_async_remote_copy(
            src_ref=src,
            dst_ref=dst,
            send_sem=halo_send.at[2 * k + field],
            recv_sem=halo_recv.at[2 * k + field],
            device_id=target,
            device_id_type=MESH,
        )

    fields = ((0, p_in, p), (1, a_in, a))
    sends = (gx < n_gx - 1, gx > 0, gy < n_gy - 1, gy > 0)
    gets = (gx > 0, gx < n_gx - 1, gy > 0, gy < n_gy - 1)
    for k in (0, 1, 2, 3):

        @pl.when(sends[k])
        def _(k=k):
            for field, array, scratch in fields:
                halo(k, field, array, scratch).start()

    each(n_gx - 1, functools.partial(signal, ready, "gx", n_gx))
    for load in loads[3:7]:
        load.wait()

    phiz_t = stacked(phiz[...])
    phiy_t = stacked(phiy[...])
    counts[...] = jnp.zeros_like(counts)
    cores[...] = jnp.zeros_like(cores)

    def observe(c, carry):
        at = pl.ds(pl.multiple_of(c * CHUNK, CHUNK), CHUNK)
        local_x = obs[0:1, at] - gx * rows
        in_y = one_hot(cols, CHUNK, obs[1:2, at] - gy * cols).astype(bf16)
        in_z = one_hot(depth, CHUNK, obs[2:3, at]).astype(bf16)
        in_x = [jnp.where(local_x == i, 1.0, 0.0).astype(bf16) for i in range(rows)]
        cells = jnp.concatenate([in_y * in_x[i] for i in range(rows)], axis=0)
        counts[...] += dot_nt(cells, in_z)
        both = dot_nn(phiz_t, in_z)
        high, low = split((both[:mz] + both[mz:]) * core[0:1, at])
        weighted = jnp.concatenate(
            [high * in_x[i] for i in range(rows)] + [low * in_x[i] for i in range(rows)], axis=0
        )
        cores[...] += dot_nt(weighted, in_y)
        return carry

    lax.fori_loop(0, obs.shape[1] // CHUNK, observe, 0)

    loads[7].wait()

    for k in (2, 3):
        place, line = ((TILE - 1, TILE), (TILE + cols, TILE + cols - 1))[k - 2]

        @pl.when(gets[k])
        def _(k=k, place=place):
            for field, array, scratch in fields:
                halo(k, field, array, scratch).wait_recv()
                scratch[1 : rows + 1, place] = arrive[k - 2, field]

        @pl.when(jnp.logical_not(gets[k]))
        def _(place=place, line=line):
            for _, _, scratch in fields:
                scratch[1 : rows + 1, place] = scratch[1 : rows + 1, line]

    def own(scratch, i):
        return scratch[i, TILE : TILE + cols]

    last = lax.broadcasted_iota(jnp.int32, (cols, depth), 1) == depth - 1

    def flat_faces(i):
        pc, ac = own(p, i), own(a, i)
        up = (pltpu.roll(pc, depth - 1, 1) - pc) * (pltpu.roll(ac, depth - 1, 1) - ac)
        up = jnp.where(last, 0.0, up)
        total = up + pltpu.roll(up, 1, 1)
        for s in (TILE - 1, TILE + 1):
            total += (p[i, s : s + cols] - pc) * (a[i, s : s + cols] - ac)
        return total

    def x_face(i, j):
        return (own(p, i) - own(p, j)) * (own(a, i) - own(a, j))

    def project(i, total):
        field = lp[i]
        cell = -0.5 * jnp.exp(field) * total - (core_weight * counts[i * cols : (i + 1) * cols]) * field
        high, low = split(cell)
        x = dot_nt(phiz_t, high)
        x = x[:mz] + x[mz:] + dot_nt(phiz_t[:mz], low)
        at = pl.ds(i * mz, mz)
        top = i * mz
        seen = cores[top : top + mz] + cores[tall + top : tall + top + mz]
        part[at] = x + core_weight * seen

    for i in range(1, rows - 1):
        project(i, flat_faces(i + 1) + x_face(i + 1, i) + x_face(i + 1, i + 2))
    edges = [flat_faces(1) + x_face(1, 2), flat_faces(rows) + x_face(rows, rows - 1)]

    for k in (0, 1):

        @pl.when(gets[k])
        def _(k=k):
            for field, array, scratch in fields:
                halo(k, field, array, scratch).wait_recv()

        @pl.when(jnp.logical_not(gets[k]))
        def _(k=k):
            for _, _, scratch in fields:
                scratch[(rows + 1) * k, TILE : TILE + cols] = own(scratch, 1 + (rows - 1) * k)

    project(0, edges[0] + x_face(1, 0))
    project(rows - 1, edges[1] + x_face(rows, rows + 1))

    high, low = split(part[...])
    y = dot_nt(phiy_t, high)
    y = y[:my] + y[my:] + dot_nt(phiy_t[:my], low)
    high, low = split(y)
    folded = dot_nn(high, kron[0]) + dot_nn(low, kron[0]) + dot_nn(high, kron[1])
    for i in range(n_gx):
        for j in range(n_gy):
            pieces[i, j] = folded[j * share_y : (j + 1) * share_y, i * width : (i + 1) * width]

    def piece(d):
        tx, ty = peer(d)
        return pltpu.make_async_remote_copy(
            src_ref=pieces.at[tx, ty],
            dst_ref=landed.at[d],
            send_sem=piece_send,
            recv_sem=piece_recv,
            device_id={"gx": tx, "gy": ty},
            device_id_type=MESH,
        )

    pl.semaphore_wait(ready, n_gx - 1)
    each(peers - 1, lambda d: piece(d + 1).start())
    landed[0] = pieces[gx, gy]
    rest = landed.at[pl.ds(1, peers - 1)]
    pltpu.make_async_copy(rest, rest, piece_recv).wait()
    total = jnp.sum(landed[...], axis=0)
    for i in range(share_x):
        out_ref[i] = total[:, i * mz : (i + 1) * mz]
    pltpu.make_async_copy(rest, rest, piece_send).wait()
    for k in (0, 1, 2, 3):

        @pl.when(sends[k])
        def _(k=k):
            for field, array, scratch in fields:
                halo(k, field, array, scratch).wait_send()


def body(pressure, adjoint, log_perm, phi_x, phi_y, phi_z, obs_cells, core_values):
    rows, cols, depth = pressure.shape
    n_gx, n_gy = lax.axis_size("gx"), lax.axis_size("gy")
    mx, my, mz = phi_x.shape[1], phi_y.shape[1], phi_z.shape[1]
    share_x, share_y = mx // n_gx, my // n_gy
    width = share_x * mz
    seen = core_values.shape[0]
    padded = (rows + 2, cols + 2 * TILE, depth)
    phi_y, phi_z = phi_y.T, phi_z.T
    cores = core_values.reshape(1, seen)
    args = (pressure, adjoint, log_perm, phi_x, phi_y, phi_z, obs_cells, cores)
    return pl.pallas_call(
        functools.partial(kernel, n_gx, n_gy),
        out_shape=jax.ShapeDtypeStruct((share_x, share_y, mz), f32),
        in_specs=[pl.BlockSpec(memory_space=pltpu.HBM)] * len(args),
        out_specs=pl.BlockSpec(memory_space=pltpu.VMEM),
        scratch_shapes=[
            pltpu.VMEM(padded, f32),
            pltpu.VMEM(padded, f32),
            pltpu.VMEM((rows, cols, depth), f32),
            pltpu.VMEM(phi_x.shape, f32),
            pltpu.VMEM(phi_y.shape, f32),
            pltpu.VMEM(phi_z.shape, f32),
            pltpu.VMEM(obs_cells.shape, jnp.int32),
            pltpu.VMEM((1, seen), f32),
            pltpu.VMEM((rows * cols, depth), f32),
            pltpu.VMEM((2 * rows * mz, cols), f32),
            pltpu.VMEM((rows * mz, cols), f32),
            pltpu.VMEM((2, rows * mz, mx * mz), bf16),
            pltpu.VMEM((2, 2, rows, depth), f32),
            pltpu.VMEM((2, 2, rows, depth), f32),
            pltpu.VMEM((n_gx, n_gy, share_y, width), f32),
            pltpu.VMEM((n_gx * n_gy, share_y, width), f32),
            pltpu.SemaphoreType.DMA((8,)),
            pltpu.SemaphoreType.DMA((8,)),
            pltpu.SemaphoreType.DMA((8,)),
            pltpu.SemaphoreType.DMA,
            pltpu.SemaphoreType.DMA,
            pltpu.SemaphoreType.REGULAR,
        ],
        compiler_params=pltpu.CompilerParams(
            collective_id=0, has_side_effects=True, vmem_limit_bytes=63 * 1024 * 1024
        ),
    )(*args)


def solution(mesh):
    placed = (
        P(("chain", "gx"), "gy", None),
        P(("chain", "gx"), "gy", None),
        P(("chain", "gx"), "gy", None),
        P("gx", None),
        P("gy", None),
        P(),
        P(None, "chain"),
        P("chain"),
    )
    return jax.shard_map(
        body, mesh=mesh, in_specs=placed, out_specs=P(("chain", "gx"), "gy", None), check_vma=False
    )
```

```python
import functools

import jax
import jax.numpy as jnp
from jax import lax
from jax.experimental import pallas as pl
from jax.experimental.pallas import tpu as pltpu
from jax.sharding import PartitionSpec as P

core_weight = 100.0
TILE = 8
CHUNK = 2048
f32, bf16, f8 = jnp.float32, jnp.bfloat16, jnp.float8_e4m3fn
SLOTS = 5
MESH = pl.DeviceIdType.MESH


def dot_nn(a, b):
    return lax.dot_general(a, b, (((1,), (0,)), ((), ())), preferred_element_type=f32)


def dot_nt(a, b):
    return lax.dot_general(a, b, (((1,), (1,)), ((), ())), preferred_element_type=f32)


def split(value):
    high = value.astype(bf16)
    return high, (value - high.astype(f32)).astype(bf16)


def one_hot(size, width, which):
    return jnp.where(lax.broadcasted_iota(jnp.int32, (size, width), 0) == which, 1.0, 0.0)


def each(count, step):
    if count <= 16:
        for i in range(count):
            step(i)
    else:
        lax.fori_loop(0, count, lambda i, c: (step(i), c)[1], 0)


def stacked(value):
    return jnp.concatenate(split(value), axis=0)


def kernel(
    n_gx, n_gy,
    p_in, a_in, lp_in, phix_in, phiy_in, phiz_in, obs_in, core_in,
    out_ref,
    p, a, lp, phix, phiy, phiz, obs, core,
    counts, cores, part, kron, leave, arrive, pieces, landed,
    load_sems, halo_send, halo_recv, piece_send, piece_recv, ready,
):
    rows, cols, depth = lp.shape
    mx, my, mz = phix.shape[1], phiy.shape[0], phiz.shape[0]
    share_x, share_y = mx // n_gx, my // n_gy
    width = share_x * mz
    gx, gy = lax.axis_index("gx"), lax.axis_index("gy")
    peers = n_gx * n_gy

    def peer(d):
        return lax.rem(gx + d // n_gy, n_gx), lax.rem(gy + d % n_gy, n_gy)

    inner = (pl.ds(1, rows), pl.ds(TILE, cols))
    loads = [
        pltpu.make_async_copy(src, dst, load_sems.at[i])
        for i, (src, dst) in enumerate(
            (
                (phix_in, phix),
                (p_in, p.at[inner]),
                (a_in, a.at[inner]),
                (phiy_in, phiy),
                (phiz_in, phiz),
                (obs_in, obs),
                (core_in, core),
                (lp_in, lp),
            )
        )
    ]
    barrier = pltpu.get_barrier_semaphore()

    sends = (gx < n_gx - 1, gx > 0, gy < n_gy - 1, gy > 0)
    gets = (gx > 0, gx < n_gx - 1, gy > 0, gy < n_gy - 1)
    beside = ({"gx": gx + 1}, {"gx": gx - 1}, {"gy": gy + 1}, {"gy": gy - 1})
    neighbours = sum(jnp.where(there, 1, 0) for there in sends)

    def greet(semaphore):
        for there, target in zip(sends, beside):

            @pl.when(there)
            def _(target=target):
                pl.semaphore_signal(semaphore, inc=1, device_id=target, device_id_type=MESH)

    rounds = n_gx + n_gy - 3

    def hear(i):
        @pl.when(i < rounds)
        def _():
            pl.semaphore_wait(ready.at[i], neighbours)

            @pl.when(i + 1 < rounds)
            def _():
                greet(ready.at[i + 1])

    greet(barrier)
    for load in loads:
        load.start()

    pl.semaphore_wait(barrier, neighbours)

    own_cols = pl.ds(TILE, cols)

    def halo(k, field, array, scratch):
        src, dst = (
            (array.at[rows - 1], scratch.at[0, own_cols]),
            (array.at[0], scratch.at[rows + 1, own_cols]),
            (leave.at[0, field], arrive.at[0, field]),
            (leave.at[1, field], arrive.at[1, field]),
        )[k]
        return pltpu.make_async_remote_copy(
            src_ref=src,
            dst_ref=dst,
            send_sem=halo_send.at[2 * k + field],
            recv_sem=halo_recv.at[2 * k + field],
            device_id=beside[k],
            device_id_type=MESH,
        )

    fields = ((0, p_in, p), (1, a_in, a))
    for k in (0, 1):

        @pl.when(sends[k])
        def _(k=k):
            for field, array, scratch in fields:
                halo(k, field, array, scratch).start()

    loads[1].wait()
    loads[2].wait()
    for field, scratch in ((0, p), (1, a)):
        leave[0, field] = scratch[1 : rows + 1, TILE + cols - 1]
        leave[1, field] = scratch[1 : rows + 1, TILE]

    for k in (2, 3):

        @pl.when(sends[k])
        def _(k=k):
            for field, array, scratch in fields:
                halo(k, field, array, scratch).start()

    if rounds > 0:
        greet(ready.at[0])
    for load in loads[3:7]:
        load.wait()

    loads[0].wait()
    tall, wide = rows * mz, mx * mz
    spread_rows = jnp.where(
        lax.broadcasted_iota(jnp.int32, (tall, rows), 0) // mz
        == lax.broadcasted_iota(jnp.int32, (tall, rows), 1),
        1.0,
        0.0,
    ).astype(bf16)
    spread_cols = jnp.where(
        lax.broadcasted_iota(jnp.int32, (mx, wide), 1) // mz
        == lax.broadcasted_iota(jnp.int32, (mx, wide), 0),
        1.0,
        0.0,
    ).astype(bf16)
    same = lax.rem(lax.broadcasted_iota(jnp.int32, (tall, wide), 0), mz) == lax.rem(
        lax.broadcasted_iota(jnp.int32, (tall, wide), 1), mz
    )
    for i, half in enumerate(split(phix[...])):
        block = dot_nn(dot_nn(spread_rows, half).astype(bf16), spread_cols)
        kron[i] = jnp.where(same, block, 0.0).astype(bf16)

    phiz_t = stacked(phiz[...])
    phiy_t = stacked(phiy[...])
    counts[...] = jnp.zeros_like(counts)
    cores[...] = jnp.zeros_like(cores)

    def observe(c):
        at = pl.ds(c * CHUNK, CHUNK)
        local_x = obs[0:1, at] - gx * rows
        in_y = one_hot(cols, CHUNK, obs[1:2, at] - gy * cols).astype(bf16)
        in_z = one_hot(depth, CHUNK, obs[2:3, at]).astype(bf16)
        in_x = [jnp.where(local_x == i, 1.0, 0.0).astype(bf16) for i in range(rows)]
        cells = jnp.concatenate([in_y * in_x[i] for i in range(rows)], axis=0)
        counts[...] += dot_nt(cells.astype(f8), in_z.astype(f8))
        both = dot_nn(phiz_t, in_z)
        high, low = split((both[:mz] + both[mz:]) * core[0:1, at])
        weighted = jnp.concatenate(
            [high * in_x[i] for i in range(rows)] + [low * in_x[i] for i in range(rows)], axis=0
        )
        cores[...] += dot_nt(weighted, in_y)


    per = -(-rounds // SLOTS)

    def hear_slot(slot):
        each(per, lambda i: hear(slot * per + i))

    for c in range(obs.shape[1] // CHUNK):
        observe(c)
        if c < 2:
            hear_slot(c)

    loads[7].wait()

    for k in (2, 3):
        place, line = ((TILE - 1, TILE), (TILE + cols, TILE + cols - 1))[k - 2]

        @pl.when(gets[k])
        def _(k=k, place=place):
            for field, array, scratch in fields:
                halo(k, field, array, scratch).wait_recv()
                scratch[1 : rows + 1, place] = arrive[k - 2, field]

        @pl.when(jnp.logical_not(gets[k]))
        def _(place=place, line=line):
            for _, _, scratch in fields:
                scratch[1 : rows + 1, place] = scratch[1 : rows + 1, line]

    def own(scratch, i):
        return scratch[i, TILE : TILE + cols]

    last = lax.broadcasted_iota(jnp.int32, (cols, depth), 1) == depth - 1

    def flat_faces(i):
        pc, ac = own(p, i), own(a, i)
        up = (pltpu.roll(pc, depth - 1, 1) - pc) * (pltpu.roll(ac, depth - 1, 1) - ac)
        up = jnp.where(last, 0.0, up)
        total = up + pltpu.roll(up, 1, 1)
        for s in (TILE - 1, TILE + 1):
            total += (p[i, s : s + cols] - pc) * (a[i, s : s + cols] - ac)
        return total

    def x_face(i, j):
        return (own(p, i) - own(p, j)) * (own(a, i) - own(a, j))

    def project(i, total):
        field = lp[i]
        cell = -0.5 * jnp.exp(field) * total - (core_weight * counts[i * cols : (i + 1) * cols]) * field
        high, low = split(cell)
        x = dot_nt(phiz_t, high)
        x = x[:mz] + x[mz:] + dot_nt(phiz_t[:mz], low)
        at = pl.ds(i * mz, mz)
        top = i * mz
        seen = cores[top : top + mz] + cores[tall + top : tall + top + mz]
        part[at] = x + core_weight * seen

    for i in range(1, rows - 1):
        project(i, flat_faces(i + 1) + x_face(i + 1, i) + x_face(i + 1, i + 2))
        if i == rows // 2 - 1:
            hear_slot(2)
    hear_slot(3)
    edges = [flat_faces(1) + x_face(1, 2), flat_faces(rows) + x_face(rows, rows - 1)]

    for k in (0, 1):

        @pl.when(gets[k])
        def _(k=k):
            for field, array, scratch in fields:
                halo(k, field, array, scratch).wait_recv()

        @pl.when(jnp.logical_not(gets[k]))
        def _(k=k):
            for _, _, scratch in fields:
                scratch[(rows + 1) * k, TILE : TILE + cols] = own(scratch, 1 + (rows - 1) * k)

    hear_slot(4)
    project(0, edges[0] + x_face(1, 0))
    project(rows - 1, edges[1] + x_face(rows, rows + 1))

    high, low = split(part[...])
    y = dot_nt(phiy_t, high)
    y = y[:my] + y[my:] + dot_nt(phiy_t[:my], low)
    high, low = split(y)
    folded = dot_nn(high, kron[0]) + dot_nn(low, kron[0]) + dot_nn(high, kron[1])
    for i in range(n_gx):
        for j in range(n_gy):
            pieces[i, j] = folded[j * share_y : (j + 1) * share_y, i * width : (i + 1) * width]

    def piece(d):
        tx, ty = peer(d)
        return pltpu.make_async_remote_copy(
            src_ref=pieces.at[tx, ty],
            dst_ref=landed.at[d],
            send_sem=piece_send,
            recv_sem=piece_recv,
            device_id={"gx": tx, "gy": ty},
            device_id_type=MESH,
        )

    each(peers - 1, lambda d: piece(d + 1).start())
    landed[0] = pieces[gx, gy]
    rest = landed.at[pl.ds(1, peers - 1)]
    pltpu.make_async_copy(rest, rest, piece_recv).wait()
    total = jnp.sum(landed[...], axis=0)
    for i in range(share_x):
        out_ref[i] = total[:, i * mz : (i + 1) * mz]
    pltpu.make_async_copy(rest, rest, piece_send).wait()
    for k in (0, 1, 2, 3):

        @pl.when(sends[k])
        def _(k=k):
            for field, array, scratch in fields:
                halo(k, field, array, scratch).wait_send()


def body(pressure, adjoint, log_perm, phi_x, phi_y, phi_z, obs_cells, core_values):
    rows, cols, depth = pressure.shape
    n_gx, n_gy = lax.axis_size("gx"), lax.axis_size("gy")
    mx, my, mz = phi_x.shape[1], phi_y.shape[1], phi_z.shape[1]
    share_x, share_y = mx // n_gx, my // n_gy
    width = share_x * mz
    seen = core_values.shape[0]
    padded = (rows + 2, cols + 2 * TILE, depth)
    phi_y, phi_z = phi_y.T, phi_z.T
    cores = core_values.reshape(1, seen)
    args = (pressure, adjoint, log_perm, phi_x, phi_y, phi_z, obs_cells, cores)
    return pl.pallas_call(
        functools.partial(kernel, n_gx, n_gy),
        out_shape=jax.ShapeDtypeStruct((share_x, share_y, mz), f32),
        in_specs=[pl.BlockSpec(memory_space=pltpu.HBM)] * len(args),
        out_specs=pl.BlockSpec(memory_space=pltpu.VMEM),
        scratch_shapes=[
            pltpu.VMEM(padded, f32),
            pltpu.VMEM(padded, f32),
            pltpu.VMEM((rows, cols, depth), f32),
            pltpu.VMEM(phi_x.shape, f32),
            pltpu.VMEM(phi_y.shape, f32),
            pltpu.VMEM(phi_z.shape, f32),
            pltpu.VMEM(obs_cells.shape, jnp.int32),
            pltpu.VMEM((1, seen), f32),
            pltpu.VMEM((rows * cols, depth), f32),
            pltpu.VMEM((2 * rows * mz, cols), f32),
            pltpu.VMEM((rows * mz, cols), f32),
            pltpu.VMEM((2, rows * mz, mx * mz), bf16),
            pltpu.VMEM((2, 2, rows, depth), f32),
            pltpu.VMEM((2, 2, rows, depth), f32),
            pltpu.VMEM((n_gx, n_gy, share_y, width), f32),
            pltpu.VMEM((n_gx * n_gy, share_y, width), f32),
            pltpu.SemaphoreType.DMA((8,)),
            pltpu.SemaphoreType.DMA((8,)),
            pltpu.SemaphoreType.DMA((8,)),
            pltpu.SemaphoreType.DMA,
            pltpu.SemaphoreType.DMA,
            pltpu.SemaphoreType.REGULAR((max(n_gx + n_gy - 3, 1),)),
        ],
        compiler_params=pltpu.CompilerParams(
            collective_id=0, has_side_effects=True, vmem_limit_bytes=63 * 1024 * 1024
        ),
    )(*args)


def solution(mesh):
    placed = (
        P(("chain", "gx"), "gy", None),
        P(("chain", "gx"), "gy", None),
        P(("chain", "gx"), "gy", None),
        P("gx", None),
        P("gy", None),
        P(),
        P(None, "chain"),
        P("chain"),
    )
    return jax.shard_map(
        body, mesh=mesh, in_specs=placed, out_specs=P(("chain", "gx"), "gy", None), check_vma=False
    )
```

```python
import functools

import jax
import jax.numpy as jnp
from jax import lax
from jax.experimental import pallas as pl
from jax.experimental.pallas import tpu as pltpu
from jax.sharding import PartitionSpec as P

core_weight = 100.0
TILE = 8
CHUNK = 2048
f32, bf16, f8 = jnp.float32, jnp.bfloat16, jnp.float8_e4m3fn
SLOTS = 5
MESH = pl.DeviceIdType.MESH


def dot_nn(a, b):
    return lax.dot_general(a, b, (((1,), (0,)), ((), ())), preferred_element_type=f32)


def dot_nt(a, b):
    return lax.dot_general(a, b, (((1,), (1,)), ((), ())), preferred_element_type=f32)


def split(value):
    high = value.astype(bf16)
    return high, (value - high.astype(f32)).astype(bf16)


def one_hot(size, width, which):
    return jnp.where(lax.broadcasted_iota(jnp.int32, (size, width), 0) == which, 1.0, 0.0)


def each(count, step):
    if count <= 16:
        for i in range(count):
            step(i)
    else:
        lax.fori_loop(0, count, lambda i, c: (step(i), c)[1], 0)


def stacked(value):
    return jnp.concatenate(split(value), axis=0)


def kernel(
    n_gx, n_gy,
    p_in, a_in, lp_in, phix_in, phiy_in, phiz_in, obs_in, core_in,
    out_ref,
    p, a, lp, phix, phiy, phiz, obs, core,
    counts, cores, part, kron, leave, arrive, pieces, landed,
    load_sems, halo_send, halo_recv, piece_send, piece_recv, ready,
):
    rows, cols, depth = lp.shape
    mx, my, mz = phix.shape[1], phiy.shape[0], phiz.shape[0]
    share_x, share_y = mx // n_gx, my // n_gy
    width = share_x * mz
    gx, gy = lax.axis_index("gx"), lax.axis_index("gy")
    peers = n_gx * n_gy

    def peer(d):
        return lax.rem(gx + d // n_gy, n_gx), lax.rem(gy + d % n_gy, n_gy)

    inner = (pl.ds(1, rows), pl.ds(TILE, cols))
    loads = [
        pltpu.make_async_copy(src, dst, load_sems.at[i])
        for i, (src, dst) in enumerate(
            (
                (phix_in, phix),
                (p_in, p.at[inner]),
                (a_in, a.at[inner]),
                (phiy_in, phiy),
                (phiz_in, phiz),
                (obs_in, obs),
                (core_in, core),
                (lp_in, lp),
            )
        )
    ]
    barrier = pltpu.get_barrier_semaphore()

    sends = (gx < n_gx - 1, gx > 0, gy < n_gy - 1, gy > 0)
    gets = (gx > 0, gx < n_gx - 1, gy > 0, gy < n_gy - 1)
    beside = ({"gx": gx + 1}, {"gx": gx - 1}, {"gy": gy + 1}, {"gy": gy - 1})
    neighbours = sum(jnp.where(there, 1, 0) for there in sends)

    def greet(semaphore):
        for there, target in zip(sends, beside):

            @pl.when(there)
            def _(target=target):
                pl.semaphore_signal(semaphore, inc=1, device_id=target, device_id_type=MESH)

    rounds = n_gx + n_gy - 3

    def hear(i):
        @pl.when(i < rounds)
        def _():
            pl.semaphore_wait(ready.at[i], neighbours)

            @pl.when(i + 1 < rounds)
            def _():
                greet(ready.at[i + 1])

    greet(barrier)
    for load in loads:
        load.start()

    pl.semaphore_wait(barrier, neighbours)

    own_cols = pl.ds(TILE, cols)

    def halo(k, field, array, scratch):
        src, dst = (
            (array.at[rows - 1], scratch.at[0, own_cols]),
            (array.at[0], scratch.at[rows + 1, own_cols]),
            (leave.at[0, field], arrive.at[0, field]),
            (leave.at[1, field], arrive.at[1, field]),
        )[k]
        return pltpu.make_async_remote_copy(
            src_ref=src,
            dst_ref=dst,
            send_sem=halo_send.at[2 * k + field],
            recv_sem=halo_recv.at[2 * k + field],
            device_id=beside[k],
            device_id_type=MESH,
        )

    fields = ((0, p_in, p), (1, a_in, a))
    for k in (0, 1):

        @pl.when(sends[k])
        def _(k=k):
            for field, array, scratch in fields:
                halo(k, field, array, scratch).start()

    loads[1].wait()
    loads[2].wait()
    for field, scratch in ((0, p), (1, a)):
        leave[0, field] = scratch[1 : rows + 1, TILE + cols - 1]
        leave[1, field] = scratch[1 : rows + 1, TILE]

    for k in (2, 3):

        @pl.when(sends[k])
        def _(k=k):
            for field, array, scratch in fields:
                halo(k, field, array, scratch).start()

    if rounds > 0:
        greet(ready.at[0])
    for load in loads[3:7]:
        load.wait()

    loads[0].wait()
    tall, wide = rows * mz, mx * mz
    spread_rows = jnp.where(
        lax.broadcasted_iota(jnp.int32, (tall, rows), 0) // mz
        == lax.broadcasted_iota(jnp.int32, (tall, rows), 1),
        1.0,
        0.0,
    ).astype(bf16)
    spread_cols = jnp.where(
        lax.broadcasted_iota(jnp.int32, (mx, wide), 1) // mz
        == lax.broadcasted_iota(jnp.int32, (mx, wide), 0),
        1.0,
        0.0,
    ).astype(bf16)
    same = lax.rem(lax.broadcasted_iota(jnp.int32, (tall, wide), 0), mz) == lax.rem(
        lax.broadcasted_iota(jnp.int32, (tall, wide), 1), mz
    )
    for i, half in enumerate(split(phix[...])):
        block = dot_nn(dot_nn(spread_rows, half).astype(bf16), spread_cols)
        kron[i] = jnp.where(same, block, 0.0).astype(bf16)

    phiz_t = stacked(phiz[...])
    phiy_t = stacked(phiy[...])
    counts[...] = jnp.zeros_like(counts)
    cores[...] = jnp.zeros_like(cores)

    def observe(c):
        at = pl.ds(c * CHUNK, CHUNK)
        local_x = obs[0:1, at] - gx * rows
        in_y = one_hot(cols, CHUNK, obs[1:2, at] - gy * cols).astype(bf16)
        in_z = one_hot(depth, CHUNK, obs[2:3, at]).astype(bf16)
        in_x = [jnp.where(local_x == i, 1.0, 0.0).astype(bf16) for i in range(rows)]
        cells = jnp.concatenate([in_y * in_x[i] for i in range(rows)], axis=0)
        counts[...] += dot_nt(cells.astype(f8), in_z.astype(f8))
        both = dot_nn(phiz_t, in_z)
        high, low = split((both[:mz] + both[mz:]) * core[0:1, at])
        weighted = jnp.concatenate(
            [high * in_x[i] for i in range(rows)] + [low * in_x[i] for i in range(rows)], axis=0
        )
        cores[...] += dot_nt(weighted, in_y)


    per = -(-rounds // SLOTS)

    def hear_slot(slot):
        each(per, lambda i: hear(slot * per + i))

    for c in range(obs.shape[1] // CHUNK):
        observe(c)
        if c < 2:
            hear_slot(c)

    loads[7].wait()

    for k in (2, 3):
        place, line = ((TILE - 1, TILE), (TILE + cols, TILE + cols - 1))[k - 2]

        @pl.when(gets[k])
        def _(k=k, place=place):
            for field, array, scratch in fields:
                halo(k, field, array, scratch).wait_recv()
                scratch[1 : rows + 1, place] = arrive[k - 2, field]

        @pl.when(jnp.logical_not(gets[k]))
        def _(place=place, line=line):
            for _, _, scratch in fields:
                scratch[1 : rows + 1, place] = scratch[1 : rows + 1, line]

    def own(scratch, i):
        return scratch[i, TILE : TILE + cols]

    last = lax.broadcasted_iota(jnp.int32, (cols, depth), 1) == depth - 1

    def flat_faces(i):
        pc, ac = own(p, i), own(a, i)
        up = (pltpu.roll(pc, depth - 1, 1) - pc) * (pltpu.roll(ac, depth - 1, 1) - ac)
        up = jnp.where(last, 0.0, up)
        total = up + pltpu.roll(up, 1, 1)
        for s in (TILE - 1, TILE + 1):
            total += (p[i, s : s + cols] - pc) * (a[i, s : s + cols] - ac)
        return total

    def x_face(i, j):
        return (own(p, i) - own(p, j)) * (own(a, i) - own(a, j))

    def project(i, total):
        field = lp[i]
        cell = -0.5 * jnp.exp(field) * total - (core_weight * counts[i * cols : (i + 1) * cols]) * field
        high, low = split(cell)
        x = dot_nt(phiz_t, high)
        x = x[:mz] + x[mz:] + dot_nt(phiz_t[:mz], low)
        at = pl.ds(i * mz, mz)
        top = i * mz
        seen = cores[top : top + mz] + cores[tall + top : tall + top + mz]
        part[at] = x + core_weight * seen

    hear_slot(2)
    for i in range(1, rows - 1):
        project(i, flat_faces(i + 1) + x_face(i + 1, i) + x_face(i + 1, i + 2))
        if i == rows // 2 - 1:
            hear_slot(3)
    edges = [flat_faces(1) + x_face(1, 2), flat_faces(rows) + x_face(rows, rows - 1)]
    hear_slot(4)

    for k in (0, 1):

        @pl.when(gets[k])
        def _(k=k):
            for field, array, scratch in fields:
                halo(k, field, array, scratch).wait_recv()

        @pl.when(jnp.logical_not(gets[k]))
        def _(k=k):
            for _, _, scratch in fields:
                scratch[(rows + 1) * k, TILE : TILE + cols] = own(scratch, 1 + (rows - 1) * k)

    project(0, edges[0] + x_face(1, 0))
    project(rows - 1, edges[1] + x_face(rows, rows + 1))

    high, low = split(part[...])
    y = dot_nt(phiy_t, high)
    y = y[:my] + y[my:] + dot_nt(phiy_t[:my], low)
    high, low = split(y)
    folded = dot_nn(high, kron[0]) + dot_nn(low, kron[0]) + dot_nn(high, kron[1])
    for i in range(n_gx):
        for j in range(n_gy):
            pieces[i, j] = folded[j * share_y : (j + 1) * share_y, i * width : (i + 1) * width]

    def piece(d):
        tx, ty = peer(d)
        return pltpu.make_async_remote_copy(
            src_ref=pieces.at[tx, ty],
            dst_ref=landed.at[d],
            send_sem=piece_send,
            recv_sem=piece_recv,
            device_id={"gx": tx, "gy": ty},
            device_id_type=MESH,
        )

    each(peers - 1, lambda d: piece(d + 1).start())
    landed[0] = pieces[gx, gy]
    rest = landed.at[pl.ds(1, peers - 1)]
    pltpu.make_async_copy(rest, rest, piece_recv).wait()
    total = jnp.sum(landed[...], axis=0)
    for i in range(share_x):
        out_ref[i] = total[:, i * mz : (i + 1) * mz]
    pltpu.make_async_copy(rest, rest, piece_send).wait()
    for k in (0, 1, 2, 3):

        @pl.when(sends[k])
        def _(k=k):
            for field, array, scratch in fields:
                halo(k, field, array, scratch).wait_send()


def body(pressure, adjoint, log_perm, phi_x, phi_y, phi_z, obs_cells, core_values):
    rows, cols, depth = pressure.shape
    n_gx, n_gy = lax.axis_size("gx"), lax.axis_size("gy")
    mx, my, mz = phi_x.shape[1], phi_y.shape[1], phi_z.shape[1]
    share_x, share_y = mx // n_gx, my // n_gy
    width = share_x * mz
    seen = core_values.shape[0]
    padded = (rows + 2, cols + 2 * TILE, depth)
    phi_y, phi_z = phi_y.T, phi_z.T
    cores = core_values.reshape(1, seen)
    args = (pressure, adjoint, log_perm, phi_x, phi_y, phi_z, obs_cells, cores)
    return pl.pallas_call(
        functools.partial(kernel, n_gx, n_gy),
        out_shape=jax.ShapeDtypeStruct((share_x, share_y, mz), f32),
        in_specs=[pl.BlockSpec(memory_space=pltpu.HBM)] * len(args),
        out_specs=pl.BlockSpec(memory_space=pltpu.VMEM),
        scratch_shapes=[
            pltpu.VMEM(padded, f32),
            pltpu.VMEM(padded, f32),
            pltpu.VMEM((rows, cols, depth), f32),
            pltpu.VMEM(phi_x.shape, f32),
            pltpu.VMEM(phi_y.shape, f32),
            pltpu.VMEM(phi_z.shape, f32),
            pltpu.VMEM(obs_cells.shape, jnp.int32),
            pltpu.VMEM((1, seen), f32),
            pltpu.VMEM((rows * cols, depth), f32),
            pltpu.VMEM((2 * rows * mz, cols), f32),
            pltpu.VMEM((rows * mz, cols), f32),
            pltpu.VMEM((2, rows * mz, mx * mz), bf16),
            pltpu.VMEM((2, 2, rows, depth), f32),
            pltpu.VMEM((2, 2, rows, depth), f32),
            pltpu.VMEM((n_gx, n_gy, share_y, width), f32),
            pltpu.VMEM((n_gx * n_gy, share_y, width), f32),
            pltpu.SemaphoreType.DMA((8,)),
            pltpu.SemaphoreType.DMA((8,)),
            pltpu.SemaphoreType.DMA((8,)),
            pltpu.SemaphoreType.DMA,
            pltpu.SemaphoreType.DMA,
            pltpu.SemaphoreType.REGULAR((max(n_gx + n_gy - 3, 1),)),
        ],
        compiler_params=pltpu.CompilerParams(
            collective_id=0, has_side_effects=True, vmem_limit_bytes=63 * 1024 * 1024
        ),
    )(*args)


def solution(mesh):
    placed = (
        P(("chain", "gx"), "gy", None),
        P(("chain", "gx"), "gy", None),
        P(("chain", "gx"), "gy", None),
        P("gx", None),
        P("gy", None),
        P(),
        P(None, "chain"),
        P("chain"),
    )
    return jax.shard_map(
        body, mesh=mesh, in_specs=placed, out_specs=P(("chain", "gx"), "gy", None), check_vma=False
    )
```
